256 devices in a mesh: mode: 16 (over x, y_lo, core), wall: 16 (over y_hi, z).
Axes of the slice: x: 4, y: 4 (y_hi: 2, y_lo: 2; y = y_hi * 2 + y_lo), z: 8, core: 2. Of those that a mesh axis runs over, the one named last changes fastest.
Arguments:
- vectors: bfloat16 [2, 2560, 8192], P(None, 'wall', 'mode'), may hold values from -6 to 6
- coupling: bfloat16 [5, 2, 2560, 2560], P(None, None, 'wall'), may hold values from -0.0390625 to 0.0390625
- pattern: int32 [5, 16, 16], replicated, may hold values 0 or 1
Outputs:
- image: bfloat16 [2, 2560, 8192], P(None, 'wall', 'mode')
The draws below stay inside these ranges and needn't reach their ends.
All inputs are finite; a program needn't handle non-finite values.
Results may differ from the reference program's by a relative error of at most 0.001.
Values may be sent and summed in bfloat16 or wider, within the bound.
No kernel may reach another device: no remote copies, remote signals or barrier semaphores. Data moves between devices by JAX's collectives and lax.ppermute only.
A program may use at most 128 MiB of HBM per device.

```python
import jax
import jax.numpy as jnp

F = 5
BLK = 32
HARM = 64
HMAX = 2
NV = 16
NOFF = 5
NCF = 2560
NB = 16
MODES = 512


def place_ends(array, key, least, largest):
    place = [jax.random.randint(jax.random.fold_in(key, axis), (), 0, length) for axis, length in enumerate(array.shape)]
    longest = array.shape.index(max(array.shape))
    neighbour = place[:longest] + [(place[longest] + 1) % array.shape[longest]] + place[longest + 1:]
    return array.at[tuple(place)].set(least).at[tuple(neighbour)].set(largest)


def block_levels(stream_key, dims, pieces, smallest, top_value):
    def one(axis_at, shards_of):
        steps = jax.random.uniform(jax.random.fold_in(jax.random.fold_in(stream_key, 6), axis_at), (shards_of,), jnp.float32, smallest / len(pieces), top_value / len(pieces))
        return jnp.repeat(jnp.exp(steps), dims[axis_at] // shards_of).reshape((-1,) + (1,) * (len(dims) - axis_at - 1))

    factor_of = one(*pieces[0])
    for cut in pieces[1:]:
        factor_of = factor_of * one(*cut)
    return factor_of


def normal_values(rng, shape, width, reach, cuts=(), dtype=jnp.bfloat16):
    drawn = jax.random.normal(rng, shape, jnp.float32) * width
    if len(cuts) > 0:
        drawn = block_levels(rng, shape, cuts, -0.22, 0.18) * drawn
    return jnp.clip(drawn, min=-reach, max=reach).astype(dtype)


def setup_inputs(seed: int = 0) -> dict:
    arg_keys = jax.random.split(jax.random.key(seed), 4)
    vectors = normal_values(arg_keys[0], (2, NCF, MODES * NV), 1.0, 6.0, ((1, 16), (2, 16)))
    coupling = normal_values(arg_keys[1], (NOFF, 2, NCF, NCF), (2 * NCF * NOFF) ** -0.5, 0.0390625, ((2, 16),))
    pattern = place_ends((jax.random.randint(arg_keys[2], (NOFF, NB, NB), 0, 4) < 3).astype(jnp.int32), jax.random.fold_in(arg_keys[2], 1), 0, 1)
    return {"vectors": vectors, "coupling": coupling, "pattern": pattern}


def expand(pattern_h):
    grown = jnp.repeat(jnp.repeat(pattern_h, BLK * F, axis=0), BLK * F, axis=1)
    return grown.T.astype(jnp.bfloat16)


def reference(vectors, coupling, pattern):
    cols = MODES * NV
    total_re = jnp.zeros((NCF, cols), jnp.float32)
    total_im = jnp.zeros((NCF, cols), jnp.float32)
    blocked = vectors.reshape(2, NCF, MODES, NV)
    for harmonic in range(NOFF):
        offset = (harmonic - HMAX) * HARM
        moved = jnp.roll(blocked, offset, axis=2).reshape(2, NCF, cols)
        part_re = moved[0]
        part_im = moved[1]
        mask = expand(pattern[harmonic])
        coup_re = coupling[harmonic, 0] * mask
        coup_im = coupling[harmonic, 1] * mask
        total_re = total_re + jnp.dot(coup_re, part_re, preferred_element_type=jnp.float32) - jnp.dot(coup_im, part_im, preferred_element_type=jnp.float32)
        total_im = total_im + jnp.dot(coup_im, part_re, preferred_element_type=jnp.float32) + jnp.dot(coup_re, part_im, preferred_element_type=jnp.float32)
    result = jnp.stack([total_re, total_im])
    return result.astype(jnp.bfloat16)
```

```python
import functools

import jax
import jax.numpy as jnp
from jax import lax
from jax.experimental import pallas as pl
from jax.experimental.pallas import tpu as pltpu
from jax.sharding import PartitionSpec as P

F = 5
BLK = 32
ROWS = F * BLK
HMAX = 2
NOFF = 2 * HMAX + 1
Q = 8
HALF = 64
TILE = 2 * HALF
CORES = 2
WALL_Z = 8
WINDOW = 256
VMEM_BYTES = 48 * 2**20

MODE = ("mode", "wall")
GROUPS = [[2 * q + core for q in range(Q)] for core in range(CORES)]


def permutation(move):
    pairs = []
    for x in range(4):
        for y_lo in range(2):
            for core in range(CORES):
                for y_hi in range(2):
                    for z in range(WALL_Z):
                        nx, ny_lo, ny_hi, nz = move(x, y_lo, y_hi, z)
                        pairs.append((
                            ((x * 2 + y_lo) * CORES + core) * 16 + y_hi * WALL_Z + z,
                            ((nx * 2 + ny_lo) * CORES + core) * 16 + ny_hi * WALL_Z + nz,
                        ))
    return pairs


UP = permutation(lambda x, y_lo, y_hi, z: (x, y_lo, y_hi, (z + 1) % WALL_Z))
DOWN = permutation(lambda x, y_lo, y_hi, z: (x, y_lo, y_hi, (z - 1) % WALL_Z))
ACROSS = permutation(lambda x, y_lo, y_hi, z: (x, 1 - y_lo, 1 - y_hi, z))


def up(value):
    return lax.ppermute(value, MODE, UP)


def down(value):
    return lax.ppermute(value, MODE, DOWN)


def across(value):
    return lax.ppermute(value, MODE, ACROSS)


def pack_kernel(flip_ref, x_ref, out_ref):
    flip = flip_ref[0]
    for c in range(Q):
        cols = slice(c * HALF, (c + 1) * HALF)
        out_ref[c ^ flip] = jnp.concatenate([x_ref[0, :, cols], x_ref[1, :, cols]], axis=1)


def unpack_kernel(flip_ref, pieces_ref, out_ref):
    flip = flip_ref[0]
    for t in range(Q // 2):
        a = pieces_ref[(2 * t) ^ flip]
        b = pieces_ref[(2 * t + 1) ^ flip]
        cols = slice(t * TILE, (t + 1) * TILE)
        out_ref[0, :, cols] = jnp.concatenate([a[:, :HALF], b[:, :HALF]], axis=1)
        out_ref[1, :, cols] = jnp.concatenate([a[:, HALF:], b[:, HALF:]], axis=1)


def small_call(kernel, flip, value, shape):
    return pl.pallas_call(
        kernel,
        out_shape=jax.ShapeDtypeStruct(shape, value.dtype),
        in_specs=[pl.BlockSpec(memory_space=pltpu.SMEM), pl.BlockSpec(memory_space=pltpu.VMEM)],
        out_specs=pl.BlockSpec(memory_space=pltpu.VMEM),
        compiler_params=pltpu.CompilerParams(vmem_limit_bytes=VMEM_BYTES),
        cost_estimate=pl.CostEstimate(flops=0, bytes_accessed=4 * value.size, transcendentals=0),
    )(flip, value)


def product_kernel(blocks, first, last, walls_ref, here_ref, pattern_ref, *refs):
    x_refs = refs[:blocks]
    e_lo_ref, e_hi_ref = refs[blocks:blocks + 2]
    rest = refs[blocks + 2:]
    if first:
        acc_ref, padded_ref = rest
    elif last:
        acc_in_ref, out_ref, padded_ref, acc_ref = rest
    else:
        acc_in_ref, acc_ref, padded_ref = rest
    step = pl.program_id(0)
    here = here_ref[0]

    @pl.when(step == 0)
    def _():
        acc_ref[...] = jnp.zeros_like(acc_ref) if first else acc_in_ref[...]

    wall = walls_ref[step]
    offset = pl.multiple_of(lax.rem(wall, 4) * 32, 32)
    padded_ref[...] = jnp.zeros_like(padded_ref)
    for j in range(blocks):
        @pl.when(step == j)
        def _():
            padded_ref[1, :, pl.ds(offset, ROWS), :] = x_refs[j][...]

    left = jnp.concatenate(
        [
            jnp.concatenate(
                [jnp.concatenate([e_lo_ref[h, part], e_hi_ref[h, part]], axis=1) for h in range(NOFF)], axis=1
            )
            for part in range(2)
        ],
        axis=0,
    )
    present = [pattern_ref[(h * 16 + wall) * 16 + here] for h in range(NOFF)]
    for pair in range(Q // 2):
        q = 2 * pair
        right = jnp.concatenate(
            [
                jnp.concatenate(
                    [padded_ref[present[h], (q + k - (h - HMAX)) % Q] for k in range(2)], axis=1
                )
                for h in range(NOFF)
            ],
            axis=0,
        )
        result = jnp.dot(left, right, preferred_element_type=jnp.float32)
        acc_ref[q] += result[:, :TILE]
        acc_ref[q + 1] += result[:, TILE:]

    if last:
        @pl.when(step == blocks - 1)
        def _():
            lane = lax.broadcasted_iota(jnp.int32, (ROWS, TILE), 1)
            for q in range(Q):
                turned = pltpu.roll(acc_ref[q, ROWS:], HALF, 1)
                total = acc_ref[q, :ROWS] + jnp.where(lane < HALF, -turned, turned)
                out_ref[q] = total.astype(out_ref.dtype)


def product(xs, walls, here, pattern, coupling, acc, last):
    blocks = len(xs)
    first = acc is None
    whole = lambda shape: pl.BlockSpec(shape, lambda s, *_: (0,) * len(shape))
    acc_shape = (Q, 2 * ROWS, TILE)
    e_shape = (NOFF, 2, ROWS, 128)
    tile_at = lambda more: lambda s, walls, *_: (0, 0, 0, walls[s] * 5 // 4 + more)
    in_specs = [whole((Q, ROWS, TILE))] * blocks + [
        pl.BlockSpec(e_shape, tile_at(0)), pl.BlockSpec(e_shape, tile_at(1))
    ]
    operands = list(xs) + [coupling, coupling]
    scratch = [pltpu.VMEM((2, Q, WINDOW, TILE), jnp.bfloat16)]
    if not first:
        in_specs.append(whole(acc_shape))
        operands.append(acc)
    if last:
        scratch.append(pltpu.VMEM(acc_shape, jnp.float32))
        out_shape, out_spec = jax.ShapeDtypeStruct((Q, ROWS, TILE), jnp.bfloat16), whole((Q, ROWS, TILE))
    else:
        out_shape, out_spec = jax.ShapeDtypeStruct(acc_shape, jnp.float32), whole(acc_shape)
    flops = blocks * 2 * NOFF * WINDOW * 2 * ROWS * Q * TILE
    return pl.pallas_call(
        functools.partial(product_kernel, blocks, first, last),
        out_shape=out_shape,
        grid_spec=pltpu.PrefetchScalarGridSpec(
            num_scalar_prefetch=3, grid=(blocks,), in_specs=in_specs, out_specs=out_spec, scratch_shapes=scratch
        ),
        compiler_params=pltpu.CompilerParams(vmem_limit_bytes=VMEM_BYTES),
        cost_estimate=pl.CostEstimate(flops=flops, bytes_accessed=blocks * 1200000 + 2600000, transcendentals=0),
    )(walls, here, pattern, *operands)


def per_device(vectors, coupling, pattern):
    wall = lax.axis_index("wall")
    y_hi, z = wall // WALL_Z, lax.rem(wall, WALL_Z)
    flip = y_hi.reshape(1).astype(jnp.int32)
    here = wall.reshape(1).astype(jnp.int32)
    pattern = pattern.reshape(-1)

    pieces = small_call(pack_kernel, flip, vectors, (Q, ROWS, TILE))
    block = lax.all_to_all(pieces, "mode", 0, 0, axis_index_groups=GROUPS, tiled=True)

    own, other = {0: block}, {}

    def walls_of(names):
        return jnp.stack([
            (y_hi if kind is own else 1 - y_hi) * WALL_Z + lax.rem(z + d + WALL_Z, WALL_Z) for kind, d in names
        ]).astype(jnp.int32)

    def add(names, acc, last=False):
        return product([kind[d] for kind, d in names], walls_of(names), here, pattern, coupling, acc, last)

    own[-1], own[1], other[0] = up(own[0]), down(own[0]), across(own[0])
    acc = add([(own, 0)], None)
    own[-2], own[2], other[1] = up(own[-1]), down(own[1]), across(own[1])
    acc = add([(own, -1), (own, 1), (other, 0)], acc)
    own[-3], own[3], other[-2] = up(own[-2]), down(own[2]), across(own[-2])
    acc = add([(own, -2), (own, 2), (other, 1)], acc)
    other[-1], other[2], other[-3] = up(other[0]), down(other[1]), across(own[-3])
    acc = add([(own, -3), (own, 3), (other, -2)], acc)
    other[4], own[4], other[3] = up(other[-3]), down(own[3]), across(own[3])
    acc = add([(other, -1), (other, 2), (other, -3)], acc)
    result = add([(other, 4), (own, 4), (other, 3)], acc, last=True)

    back = lax.all_to_all(result, "mode", 0, 0, axis_index_groups=GROUPS, tiled=True)
    return small_call(unpack_kernel, flip, back, vectors.shape)


def solution(mesh):
    placed = (P(None, "wall", "mode"), P(None, None, "wall", None), P())
    return jax.shard_map(
        per_device, mesh=mesh, in_specs=placed, out_specs=P(None, "wall", "mode"), check_vma=False
    )
```

```python
import functools

import jax
import jax.numpy as jnp
from jax import lax
from jax.experimental import pallas as pl
from jax.experimental.pallas import tpu as pltpu
from jax.sharding import PartitionSpec as P

F = 5
BLK = 32
ROWS = F * BLK
HMAX = 2
NOFF = 2 * HMAX + 1
Q = 8
HALF = 64
TILE = 2 * HALF
CORES = 2
WALL_Z = 8
WALLS = 16
RUN = 4
WINDOW = 768
HALF_TILES = 10
RING_TILES = 14
VMEM_BYTES = 24 * 2**20

MODE = ("mode", "wall")
GROUPS = [[2 * q + core for q in range(Q)] for core in range(CORES)]


def permutation(move):
    pairs = []
    for x in range(4):
        for y_lo in range(2):
            for core in range(CORES):
                for y_hi in range(2):
                    for z in range(WALL_Z):
                        nx, ny_lo, ny_hi, nz = move(x, y_lo, y_hi, z)
                        pairs.append((
                            ((x * 2 + y_lo) * CORES + core) * 16 + y_hi * WALL_Z + z,
                            ((nx * 2 + ny_lo) * CORES + core) * 16 + ny_hi * WALL_Z + nz,
                        ))
    return pairs


UP = permutation(lambda x, y_lo, y_hi, z: (x, y_lo, y_hi, (z + 1) % WALL_Z))
DOWN = permutation(lambda x, y_lo, y_hi, z: (x, y_lo, y_hi, (z - 1) % WALL_Z))
ACROSS = permutation(lambda x, y_lo, y_hi, z: (x, 1 - y_lo, 1 - y_hi, z))
ACROSS_DOWN = permutation(lambda x, y_lo, y_hi, z: (x, 1 - y_lo, 1 - y_hi, (z - 1) % WALL_Z))


def up(value):
    return lax.ppermute(value, MODE, UP)


def down(value):
    return lax.ppermute(value, MODE, DOWN)


def across(value):
    return lax.ppermute(value, MODE, ACROSS)


def across_down(value):
    return lax.ppermute(value, MODE, ACROSS_DOWN)


def pack_kernel(flip_ref, x_ref, out_ref):
    flip = flip_ref[0]
    for c in range(Q):
        cols = slice(c * HALF, (c + 1) * HALF)
        out_ref[c ^ flip] = jnp.concatenate([x_ref[0, :, cols], x_ref[1, :, cols]], axis=1)


def unpack_kernel(flip_ref, pieces_ref, out_ref):
    flip = flip_ref[0]
    for t in range(Q // 2):
        a = pieces_ref[(2 * t) ^ flip]
        b = pieces_ref[(2 * t + 1) ^ flip]
        cols = slice(t * TILE, (t + 1) * TILE)
        out_ref[0, :, cols] = jnp.concatenate([a[:, :HALF], b[:, :HALF]], axis=1)
        out_ref[1, :, cols] = jnp.concatenate([a[:, HALF:], b[:, HALF:]], axis=1)


def small_call(kernel, flip, value, shape):
    return pl.pallas_call(
        kernel,
        out_shape=jax.ShapeDtypeStruct(shape, value.dtype),
        in_specs=[pl.BlockSpec(memory_space=pltpu.SMEM), pl.BlockSpec(memory_space=pltpu.VMEM)],
        out_specs=pl.BlockSpec(memory_space=pltpu.VMEM),
        compiler_params=pltpu.CompilerParams(vmem_limit_bytes=VMEM_BYTES),
        cost_estimate=pl.CostEstimate(flops=0, bytes_accessed=4 * value.size, transcendentals=0),
    )(flip, value)


def mask_kernel(here_ref, pattern_ref, e_ref, out_ref, held_ref, sems):
    here = here_ref[0]
    lane = lax.broadcasted_iota(jnp.int32, (1, 128), 1)
    copies = [pltpu.make_async_copy(e_ref.at[h], held_ref.at[h], sems.at[h]) for h in range(NOFF)]
    for copy in copies:
        copy.start()
    for h in range(NOFF):
        copies[h].wait()
        for t in range(WALLS * ROWS // 128):
            low = t * 128 // ROWS
            high = (t * 128 + 127) // ROWS
            present = pattern_ref[(h * WALLS + low) * WALLS + here]
            if high > low:
                after = pattern_ref[(h * WALLS + high) * WALLS + here]
                present = jnp.where(lane < high * ROWS - t * 128, present, after)
            else:
                present = jnp.broadcast_to(present, (1, 128))
            mask = present.astype(jnp.float32).astype(jnp.bfloat16)
            half, at = t // HALF_TILES, t % HALF_TILES
            for part in range(2):
                value = held_ref[h, part, :, t * 128:(t + 1) * 128] * mask
                out_ref[half, h, part, :, at * 128:(at + 1) * 128] = value
                if at + HALF_TILES < RING_TILES:
                    out_ref[half, h, part, :, (at + HALF_TILES) * 128:(at + HALF_TILES + 1) * 128] = value


def masked_ring(here, pattern, coupling):
    smem = pl.BlockSpec(memory_space=pltpu.SMEM)
    return pl.pallas_call(
        mask_kernel,
        out_shape=jax.ShapeDtypeStruct((2, NOFF, 2, ROWS, RING_TILES * 128), coupling.dtype),
        in_specs=[smem, smem, pl.BlockSpec(memory_space=pltpu.HBM)],
        out_specs=pl.BlockSpec(memory_space=pltpu.VMEM),
        scratch_shapes=[pltpu.VMEM(coupling.shape, coupling.dtype), pltpu.SemaphoreType.DMA((NOFF,))],
        compiler_params=pltpu.CompilerParams(vmem_limit_bytes=VMEM_BYTES),
        cost_estimate=pl.CostEstimate(flops=0, bytes_accessed=8 * 2**20, transcendentals=0),
    )(here, pattern, pltpu.with_memory_space_constraint(coupling, pltpu.HBM))


def run_kernel(far, start, first, last, here_ref, e_ref, *refs):
    x_refs, rest = refs[:RUN], refs[RUN:]
    if first:
        out_ref, padded_ref = rest
    else:
        acc_ref, out_ref, padded_ref = rest
    here = here_ref[0]
    y_hi, z = here // WALL_Z, lax.rem(here, WALL_Z)
    half = 1 - y_hi if far else y_hi
    begin = lax.rem(z + start + WALL_Z, WALL_Z)
    offset = pl.multiple_of(lax.rem(begin, 4) * 32, 32)
    lanes = pl.multiple_of(begin * 5 // 4 * 128, 128)
    padded_ref[:, :128, :] = jnp.zeros((Q, 128, TILE), jnp.bfloat16)
    padded_ref[:, WINDOW - 128:, :] = jnp.zeros((Q, 128, TILE), jnp.bfloat16)
    for j in range(RUN):
        padded_ref[:, pl.ds(pl.multiple_of(offset + j * ROWS, 32), ROWS), :] = x_refs[j][...]
    left = jnp.concatenate(
        [
            jnp.concatenate([e_ref[half, h, part, :, pl.ds(lanes, WINDOW)] for h in range(NOFF)], axis=1)
            for part in range(2)
        ],
        axis=0,
    )
    lane = lax.broadcasted_iota(jnp.int32, (ROWS, TILE), 1)
    for pair in range(Q // 2):
        q = 2 * pair
        right = jnp.concatenate(
            [
                jnp.concatenate([padded_ref[(q + k - (h - HMAX)) % Q] for k in range(2)], axis=1)
                for h in range(NOFF)
            ],
            axis=0,
        )
        result = jnp.dot(left, right, preferred_element_type=jnp.float32)
        for k in range(2):
            part = result[:, k * TILE:(k + 1) * TILE]
            if not first:
                part = acc_ref[q + k] + part
            if last:
                turned = pltpu.roll(part[ROWS:], HALF, 1)
                part = (part[:ROWS] + jnp.where(lane < HALF, -turned, turned)).astype(out_ref.dtype)
            out_ref[q + k] = part


def run_product(xs, far, start, here, ring, acc, last=False):
    first = acc is None
    vmem, smem = pl.BlockSpec(memory_space=pltpu.VMEM), pl.BlockSpec(memory_space=pltpu.SMEM)
    operands = [here, ring, *xs] + ([] if first else [acc])
    if last:
        out_shape = jax.ShapeDtypeStruct((Q, ROWS, TILE), jnp.bfloat16)
    else:
        out_shape = jax.ShapeDtypeStruct((Q, 2 * ROWS, TILE), jnp.float32)
    return pl.pallas_call(
        functools.partial(run_kernel, far, start, first, last),
        out_shape=out_shape,
        in_specs=[smem] + [vmem] * (len(operands) - 1),
        out_specs=vmem,
        scratch_shapes=[pltpu.VMEM((Q, WINDOW, TILE), jnp.bfloat16)],
        compiler_params=pltpu.CompilerParams(vmem_limit_bytes=VMEM_BYTES),
        cost_estimate=pl.CostEstimate(
            flops=2 * NOFF * WINDOW * 2 * ROWS * Q * TILE, bytes_accessed=3 * 2**20, transcendentals=0
        ),
    )(*operands)


def per_device(vectors, coupling, pattern):
    wall = lax.axis_index("wall")
    flip = (wall // WALL_Z).reshape(1).astype(jnp.int32)
    here = wall.reshape(1).astype(jnp.int32)
    pattern = pattern.reshape(-1)
    tie = lax.optimization_barrier

    pieces = small_call(pack_kernel, flip, vectors, (Q, ROWS, TILE))
    block = lax.all_to_all(pieces, "mode", 0, 0, axis_index_groups=GROUPS, tiled=True)

    own, other = {0: block}, {}

    def add(far, start, acc, last=False):
        kind = other if far else own
        xs = [kind[(start + j + 3) % WALL_Z - 3] for j in range(RUN)]
        return run_product(xs, far, start, here, ring, acc, last)

    own[1], own[-1], other[0] = down(own[0]), up(own[0]), across(own[0])
    ring = masked_ring(here, pattern, coupling)
    own[1], ring = tie((own[1], ring))
    own[2], other[1] = down(own[1]), across(own[1])
    own[-1], other[0] = tie((own[-1], other[0]))
    own[-2] = up(own[-1])
    own[3] = down(own[2])
    other[-2] = across(own[-2])
    own[-2], other[1] = tie((own[-2], other[1]))
    own[-3] = up(own[-2])
    other[-1] = up(other[0])
    other[2] = down(other[1])
    acc = add(0, -2, None)
    own[3], acc = tie((own[3], acc))
    own[4], other[3], other[4] = down(own[3]), across(own[3]), across_down(own[3])
    other[-3] = up(other[-2])
    acc = add(1, -2, acc)
    acc = add(0, 2, acc)
    result = add(1, 2, acc, last=True)

    back = lax.all_to_all(result, "mode", 0, 0, axis_index_groups=GROUPS, tiled=True)
    return small_call(unpack_kernel, flip, back, vectors.shape)


def solution(mesh):
    placed = (P(None, "wall", "mode"), P(None, None, "wall", None), P())
    return jax.shard_map(
        per_device, mesh=mesh, in_specs=placed, out_specs=P(None, "wall", "mode"), check_vma=False
    )
```

```python
import functools

import jax
import jax.numpy as jnp
from jax import lax
from jax.experimental import pallas as pl
from jax.experimental.pallas import tpu as pltpu
from jax.sharding import PartitionSpec as P

F = 5
BLK = 32
ROWS = F * BLK
HMAX = 2
NOFF = 2 * HMAX + 1
Q = 8
HALF = 64
TILE = 2 * HALF
CORES = 2
WALL_Z = 8
WALLS = 16
RUN = 4
WINDOW = 768
HALF_TILES = 10
RING_TILES = 14
VMEM_BYTES = 24 * 2**20

MODE = ("mode", "wall")
GROUPS = [[2 * q + core for q in range(Q)] for core in range(CORES)]


def permutation(move):
    pairs = []
    for x in range(4):
        for y_lo in range(2):
            for core in range(CORES):
                for y_hi in range(2):
                    for z in range(WALL_Z):
                        nx, ny_lo, ny_hi, nz = move(x, y_lo, y_hi, z)
                        pairs.append((
                            ((x * 2 + y_lo) * CORES + core) * 16 + y_hi * WALL_Z + z,
                            ((nx * 2 + ny_lo) * CORES + core) * 16 + ny_hi * WALL_Z + nz,
                        ))
    return pairs


UP = permutation(lambda x, y_lo, y_hi, z: (x, y_lo, y_hi, (z + 1) % WALL_Z))
DOWN = permutation(lambda x, y_lo, y_hi, z: (x, y_lo, y_hi, (z - 1) % WALL_Z))
ACROSS = permutation(lambda x, y_lo, y_hi, z: (x, 1 - y_lo, 1 - y_hi, z))
ACROSS_DOWN = permutation(lambda x, y_lo, y_hi, z: (x, 1 - y_lo, 1 - y_hi, (z - 1) % WALL_Z))


def up(value):
    return lax.ppermute(value, MODE, UP)


def down(value):
    return lax.ppermute(value, MODE, DOWN)


def across(value):
    return lax.ppermute(value, MODE, ACROSS)


def across_down(value):
    return lax.ppermute(value, MODE, ACROSS_DOWN)


def pack_kernel(flip_ref, x_ref, out_ref):
    flip = flip_ref[0]
    for c in range(Q):
        cols = slice(c * HALF, (c + 1) * HALF)
        out_ref[c ^ flip] = jnp.concatenate([x_ref[0, :, cols], x_ref[1, :, cols]], axis=1)


def unpack_kernel(flip_ref, pieces_ref, out_ref):
    flip = flip_ref[0]
    for t in range(Q // 2):
        a = pieces_ref[(2 * t) ^ flip]
        b = pieces_ref[(2 * t + 1) ^ flip]
        cols = slice(t * TILE, (t + 1) * TILE)
        out_ref[0, :, cols] = jnp.concatenate([a[:, :HALF], b[:, :HALF]], axis=1)
        out_ref[1, :, cols] = jnp.concatenate([a[:, HALF:], b[:, HALF:]], axis=1)


def small_call(kernel, flip, value, shape):
    return pl.pallas_call(
        kernel,
        out_shape=jax.ShapeDtypeStruct(shape, value.dtype),
        in_specs=[pl.BlockSpec(memory_space=pltpu.SMEM), pl.BlockSpec(memory_space=pltpu.VMEM)],
        out_specs=pl.BlockSpec(memory_space=pltpu.VMEM),
        compiler_params=pltpu.CompilerParams(vmem_limit_bytes=VMEM_BYTES),
        cost_estimate=pl.CostEstimate(flops=0, bytes_accessed=4 * value.size, transcendentals=0),
    )(flip, value)


def mask_kernel(here_ref, pattern_ref, e_ref, out_ref, held_ref, sems):
    here = here_ref[0]
    lane = lax.broadcasted_iota(jnp.int32, (1, 128), 1)
    copies = [pltpu.make_async_copy(e_ref.at[h], held_ref.at[h], sems.at[h]) for h in range(NOFF)]
    for copy in copies:
        copy.start()
    for h in range(NOFF):
        copies[h].wait()
        for t in range(WALLS * ROWS // 128):
            low = t * 128 // ROWS
            high = (t * 128 + 127) // ROWS
            present = pattern_ref[(h * WALLS + low) * WALLS + here]
            if high > low:
                after = pattern_ref[(h * WALLS + high) * WALLS + here]
                present = jnp.where(lane < high * ROWS - t * 128, present, after)
            else:
                present = jnp.broadcast_to(present, (1, 128))
            mask = present.astype(jnp.float32).astype(jnp.bfloat16)
            half, at = t // HALF_TILES, t % HALF_TILES
            for part in range(2):
                value = held_ref[h, part, :, t * 128:(t + 1) * 128] * mask
                out_ref[half, h, part, :, at * 128:(at + 1) * 128] = value
                if at + HALF_TILES < RING_TILES:
                    out_ref[half, h, part, :, (at + HALF_TILES) * 128:(at + HALF_TILES + 1) * 128] = value


def masked_ring(here, pattern, coupling):
    smem = pl.BlockSpec(memory_space=pltpu.SMEM)
    return pl.pallas_call(
        mask_kernel,
        out_shape=jax.ShapeDtypeStruct((2, NOFF, 2, ROWS, RING_TILES * 128), coupling.dtype),
        in_specs=[smem, smem, pl.BlockSpec(memory_space=pltpu.HBM)],
        out_specs=pl.BlockSpec(memory_space=pltpu.VMEM),
        scratch_shapes=[pltpu.VMEM(coupling.shape, coupling.dtype), pltpu.SemaphoreType.DMA((NOFF,))],
        compiler_params=pltpu.CompilerParams(vmem_limit_bytes=VMEM_BYTES),
        cost_estimate=pl.CostEstimate(flops=0, bytes_accessed=8 * 2**20, transcendentals=0),
    )(here, pattern, pltpu.with_memory_space_constraint(coupling, pltpu.HBM))


def run_kernel(far, start, first, last, here_ref, e_ref, *refs):
    x_refs, rest = refs[:RUN], refs[RUN:]
    if first:
        out_ref, padded_ref = rest
    else:
        acc_ref, out_ref, padded_ref = rest
    here = here_ref[0]
    y_hi, z = here // WALL_Z, lax.rem(here, WALL_Z)
    half = 1 - y_hi if far else y_hi
    begin = lax.rem(z + start + WALL_Z, WALL_Z)
    offset = pl.multiple_of(lax.rem(begin, 4) * 32, 32)
    lanes = pl.multiple_of(begin * 5 // 4 * 128, 128)
    padded_ref[:, :128, :] = jnp.zeros((Q, 128, TILE), jnp.bfloat16)
    padded_ref[:, WINDOW - 128:, :] = jnp.zeros((Q, 128, TILE), jnp.bfloat16)
    for j in range(RUN):
        padded_ref[:, pl.ds(pl.multiple_of(offset + j * ROWS, 32), ROWS), :] = x_refs[j][...]
    left = jnp.concatenate(
        [
            jnp.concatenate([e_ref[half, h, part, :, pl.ds(lanes, WINDOW)] for h in range(NOFF)], axis=1)
            for part in range(2)
        ],
        axis=0,
    )
    lane = lax.broadcasted_iota(jnp.int32, (ROWS, TILE), 1)
    for pair in range(Q // 2):
        q = 2 * pair
        right = jnp.concatenate(
            [
                jnp.concatenate([padded_ref[(q + k - (h - HMAX)) % Q] for k in range(2)], axis=1)
                for h in range(NOFF)
            ],
            axis=0,
        )
        result = jnp.dot(left, right, preferred_element_type=jnp.float32)
        for k in range(2):
            part = result[:, k * TILE:(k + 1) * TILE]
            if not first:
                part = acc_ref[q + k] + part
            if last:
                turned = pltpu.roll(part[ROWS:], HALF, 1)
                part = (part[:ROWS] + jnp.where(lane < HALF, -turned, turned)).astype(out_ref.dtype)
            out_ref[q + k] = part


def run_product(xs, far, start, here, ring, acc, last=False):
    first = acc is None
    vmem, smem = pl.BlockSpec(memory_space=pltpu.VMEM), pl.BlockSpec(memory_space=pltpu.SMEM)
    operands = [here, ring, *xs] + ([] if first else [acc])
    if last:
        out_shape = jax.ShapeDtypeStruct((Q, ROWS, TILE), jnp.bfloat16)
    else:
        out_shape = jax.ShapeDtypeStruct((Q, 2 * ROWS, TILE), jnp.float32)
    return pl.pallas_call(
        functools.partial(run_kernel, far, start, first, last),
        out_shape=out_shape,
        in_specs=[smem] + [vmem] * (len(operands) - 1),
        out_specs=vmem,
        scratch_shapes=[pltpu.VMEM((Q, WINDOW, TILE), jnp.bfloat16)],
        compiler_params=pltpu.CompilerParams(vmem_limit_bytes=VMEM_BYTES),
        cost_estimate=pl.CostEstimate(
            flops=2 * NOFF * WINDOW * 2 * ROWS * Q * TILE, bytes_accessed=3 * 2**20, transcendentals=0
        ),
    )(*operands)


def per_device(vectors, coupling, pattern):
    wall = lax.axis_index("wall")
    flip = (wall // WALL_Z).reshape(1).astype(jnp.int32)
    here = wall.reshape(1).astype(jnp.int32)
    pattern = pattern.reshape(-1)
    tie = lax.optimization_barrier

    pieces = small_call(pack_kernel, flip, vectors, (Q, ROWS, TILE))
    block = lax.all_to_all(pieces, "mode", 0, 0, axis_index_groups=GROUPS, tiled=True)

    own, other = {0: block}, {}

    def add(far, start, acc, last=False):
        kind = other if far else own
        xs = [kind[(start + j + 3) % WALL_Z - 3] for j in range(RUN)]
        return run_product(xs, far, start, here, ring, acc, last)

    own[1], own[-1], other[0] = down(own[0]), up(own[0]), across(own[0])
    ring = masked_ring(here, pattern, coupling)
    own[1], ring = tie((own[1], ring))
    own[2], own[-2] = down(own[1]), up(own[-1])
    own[1], other[0] = tie((own[1], other[0]))
    other[1] = across(own[1])
    own[3] = down(own[2])
    other[-2] = across(own[-2])
    own[-2], other[1] = tie((own[-2], other[1]))
    own[-3] = up(own[-2])
    other[-1] = up(other[0])
    other[2] = down(other[1])
    own[4], other[3], other[4] = down(own[3]), across(own[3]), across_down(own[3])
    other[-3] = up(other[-2])
    acc = add(1, -2, None)
    acc = add(0, -2, acc)
    acc = add(0, 2, acc)
    result = add(1, 2, acc, last=True)

    back = lax.all_to_all(result, "mode", 0, 0, axis_index_groups=GROUPS, tiled=True)
    return small_call(unpack_kernel, flip, back, vectors.shape)


def solution(mesh):
    placed = (P(None, "wall", "mode"), P(None, None, "wall", None), P())
    return jax.shard_map(
        per_device, mesh=mesh, in_specs=placed, out_specs=P(None, "wall", "mode"), check_vma=False
    )
```

```python
import functools

import jax
import jax.numpy as jnp
from jax import lax
from jax.experimental import pallas as pl
from jax.experimental.pallas import tpu as pltpu
from jax.sharding import PartitionSpec as P

F = 5
BLK = 32
ROWS = F * BLK
HMAX = 2
NOFF = 2 * HMAX + 1
Q = 8
HALF = 64
PIECE = ROWS // 2
TILE = 2 * HALF
CORES = 2
WALL_Z = 8
WALLS = 16
RUN = 4
WINDOW = 768
HALF_TILES = 10
RING_TILES = 14
VMEM_BYTES = 24 * 2**20

MODE = ("mode", "wall")
GROUPS = [[2 * q + core for q in range(Q)] for core in range(CORES)]


def permutation(move):
    pairs = []
    for x in range(4):
        for y_lo in range(2):
            for core in range(CORES):
                for y_hi in range(2):
                    for z in range(WALL_Z):
                        nx, ny_lo, ny_hi, nz = move(x, y_lo, y_hi, z)
                        pairs.append((
                            ((x * 2 + y_lo) * CORES + core) * 16 + y_hi * WALL_Z + z,
                            ((nx * 2 + ny_lo) * CORES + core) * 16 + ny_hi * WALL_Z + nz,
                        ))
    return pairs


UP = permutation(lambda x, y_lo, y_hi, z: (x, y_lo, y_hi, (z + 1) % WALL_Z))
DOWN = permutation(lambda x, y_lo, y_hi, z: (x, y_lo, y_hi, (z - 1) % WALL_Z))
ACROSS = permutation(lambda x, y_lo, y_hi, z: (x, 1 - y_lo, 1 - y_hi, z))
ACROSS_DOWN = permutation(lambda x, y_lo, y_hi, z: (x, 1 - y_lo, 1 - y_hi, (z - 1) % WALL_Z))


def up(value):
    return lax.ppermute(value, MODE, UP)


def down(value):
    return lax.ppermute(value, MODE, DOWN)


def across(value):
    return lax.ppermute(value, MODE, ACROSS)


def across_down(value):
    return lax.ppermute(value, MODE, ACROSS_DOWN)


def pack_kernel(flip_ref, x_ref, out_ref, held_ref, sems):
    flip = flip_ref[0]
    copies = [
        [
            pltpu.make_async_copy(
                x_ref.at[part, pl.ds(at * PIECE, PIECE)], held_ref.at[part, pl.ds(at * PIECE, PIECE)], sems.at[part, at]
            )
            for part in range(2)
        ]
        for at in range(2)
    ]
    for pair in copies:
        for copy in pair:
            copy.start()
    for at, pair in enumerate(copies):
        for copy in pair:
            copy.wait()
        rows = slice(at * PIECE, (at + 1) * PIECE)
        for c in range(Q):
            cols = slice(c * HALF, (c + 1) * HALF)
            out_ref[c ^ flip, rows, :] = jnp.concatenate([held_ref[0, rows, cols], held_ref[1, rows, cols]], axis=1)


def unpack_kernel(flip_ref, pieces_ref, out_ref, held_ref, sems):
    flip = flip_ref[0]
    copies = [pltpu.make_async_copy(held_ref.at[part], out_ref.at[part], sems.at[part]) for part in range(2)]
    for part in range(2):
        lanes = slice(part * HALF, (part + 1) * HALF)
        for t in range(Q // 2):
            a = pieces_ref[(2 * t) ^ flip]
            b = pieces_ref[(2 * t + 1) ^ flip]
            held_ref[part, :, t * TILE:(t + 1) * TILE] = jnp.concatenate([a[:, lanes], b[:, lanes]], axis=1)
        copies[part].start()
    for copy in copies:
        copy.wait()


def small_call(kernel, flip, value, shape, spaces, held, sems):
    return pl.pallas_call(
        kernel,
        out_shape=jax.ShapeDtypeStruct(shape, value.dtype),
        in_specs=[pl.BlockSpec(memory_space=pltpu.SMEM), pl.BlockSpec(memory_space=spaces[0])],
        out_specs=pl.BlockSpec(memory_space=spaces[1]),
        scratch_shapes=[pltpu.VMEM(held, value.dtype), pltpu.SemaphoreType.DMA(sems)],
        compiler_params=pltpu.CompilerParams(vmem_limit_bytes=VMEM_BYTES),
        cost_estimate=pl.CostEstimate(flops=0, bytes_accessed=4 * value.size, transcendentals=0),
    )(flip, value)


def mask_kernel(here_ref, pattern_ref, e_ref, out_ref, held_ref, sems):
    here = here_ref[0]
    lane = lax.broadcasted_iota(jnp.int32, (1, 128), 1)
    copies = [pltpu.make_async_copy(e_ref.at[h], held_ref.at[h], sems.at[h]) for h in range(NOFF)]
    for copy in copies:
        copy.start()
    for h in range(NOFF):
        copies[h].wait()
        for t in range(WALLS * ROWS // 128):
            low = t * 128 // ROWS
            high = (t * 128 + 127) // ROWS
            present = pattern_ref[(h * WALLS + low) * WALLS + here]
            if high > low:
                after = pattern_ref[(h * WALLS + high) * WALLS + here]
                present = jnp.where(lane < high * ROWS - t * 128, present, after)
            else:
                present = jnp.broadcast_to(present, (1, 128))
            mask = present.astype(jnp.float32).astype(jnp.bfloat16)
            half, at = t // HALF_TILES, t % HALF_TILES
            for part in range(2):
                value = held_ref[h, part, :, t * 128:(t + 1) * 128] * mask
                out_ref[half, h, part, :, at * 128:(at + 1) * 128] = value
                if at + HALF_TILES < RING_TILES:
                    out_ref[half, h, part, :, (at + HALF_TILES) * 128:(at + HALF_TILES + 1) * 128] = value


def masked_ring(here, pattern, coupling):
    smem = pl.BlockSpec(memory_space=pltpu.SMEM)
    return pl.pallas_call(
        mask_kernel,
        out_shape=jax.ShapeDtypeStruct((2, NOFF, 2, ROWS, RING_TILES * 128), coupling.dtype),
        in_specs=[smem, smem, pl.BlockSpec(memory_space=pltpu.HBM)],
        out_specs=pl.BlockSpec(memory_space=pltpu.VMEM),
        scratch_shapes=[pltpu.VMEM(coupling.shape, coupling.dtype), pltpu.SemaphoreType.DMA((NOFF,))],
        compiler_params=pltpu.CompilerParams(vmem_limit_bytes=VMEM_BYTES),
        cost_estimate=pl.CostEstimate(flops=0, bytes_accessed=8 * 2**20, transcendentals=0),
    )(here, pattern, pltpu.with_memory_space_constraint(coupling, pltpu.HBM))


def run_kernel(far, start, first, last, here_ref, e_ref, *refs):
    x_refs, rest = refs[:RUN], refs[RUN:]
    if first:
        out_ref, padded_ref = rest
    else:
        acc_ref, out_ref, padded_ref = rest
    here = here_ref[0]
    y_hi, z = here // WALL_Z, lax.rem(here, WALL_Z)
    half = 1 - y_hi if far else y_hi
    begin = lax.rem(z + start + WALL_Z, WALL_Z)
    offset = pl.multiple_of(lax.rem(begin, 4) * 32, 32)
    lanes = pl.multiple_of(begin * 5 // 4 * 128, 128)
    padded_ref[:, :128, :] = jnp.zeros((Q, 128, TILE), jnp.bfloat16)
    padded_ref[:, WINDOW - 128:, :] = jnp.zeros((Q, 128, TILE), jnp.bfloat16)
    for j in range(RUN):
        padded_ref[:, pl.ds(pl.multiple_of(offset + j * ROWS, 32), ROWS), :] = x_refs[j][...]
    left = jnp.concatenate(
        [
            jnp.concatenate([e_ref[half, h, part, :, pl.ds(lanes, WINDOW)] for h in range(NOFF)], axis=1)
            for part in range(2)
        ],
        axis=0,
    )
    lane = lax.broadcasted_iota(jnp.int32, (ROWS, TILE), 1)
    for pair in range(Q // 2):
        q = 2 * pair
        right = jnp.concatenate(
            [
                jnp.concatenate([padded_ref[(q + k - (h - HMAX)) % Q] for k in range(2)], axis=1)
                for h in range(NOFF)
            ],
            axis=0,
        )
        result = jnp.dot(left, right, preferred_element_type=jnp.float32)
        for k in range(2):
            part = result[:, k * TILE:(k + 1) * TILE]
            if not first:
                part = acc_ref[q + k] + part
            if last:
                turned = pltpu.roll(part[ROWS:], HALF, 1)
                part = (part[:ROWS] + jnp.where(lane < HALF, -turned, turned)).astype(out_ref.dtype)
            out_ref[q + k] = part


def run_product(xs, far, start, here, ring, acc, last=False):
    first = acc is None
    vmem, smem = pl.BlockSpec(memory_space=pltpu.VMEM), pl.BlockSpec(memory_space=pltpu.SMEM)
    operands = [here, ring, *xs] + ([] if first else [acc])
    if last:
        out_shape = jax.ShapeDtypeStruct((Q, ROWS, TILE), jnp.bfloat16)
    else:
        out_shape = jax.ShapeDtypeStruct((Q, 2 * ROWS, TILE), jnp.float32)
    return pl.pallas_call(
        functools.partial(run_kernel, far, start, first, last),
        out_shape=out_shape,
        in_specs=[smem] + [vmem] * (len(operands) - 1),
        out_specs=vmem,
        scratch_shapes=[pltpu.VMEM((Q, WINDOW, TILE), jnp.bfloat16)],
        compiler_params=pltpu.CompilerParams(vmem_limit_bytes=VMEM_BYTES),
        cost_estimate=pl.CostEstimate(
            flops=2 * NOFF * WINDOW * 2 * ROWS * Q * TILE, bytes_accessed=3 * 2**20, transcendentals=0
        ),
    )(*operands)


def per_device(vectors, coupling, pattern):
    wall = lax.axis_index("wall")
    flip = (wall // WALL_Z).reshape(1).astype(jnp.int32)
    here = wall.reshape(1).astype(jnp.int32)
    pattern = pattern.reshape(-1)
    tie = lax.optimization_barrier

    far_vectors = pltpu.with_memory_space_constraint(vectors, pltpu.HBM)
    hbm, vmem = pltpu.HBM, pltpu.VMEM
    pieces = small_call(pack_kernel, flip, far_vectors, (Q, ROWS, TILE), (hbm, vmem), vectors.shape, (2, 2))
    block = lax.all_to_all(pieces, "mode", 0, 0, axis_index_groups=GROUPS, tiled=True)

    own, other = {0: block}, {}

    def add(far, start, acc, last=False):
        kind = other if far else own
        xs = [kind[(start + j + 3) % WALL_Z - 3] for j in range(RUN)]
        return run_product(xs, far, start, here, ring, acc, last)

    own[1], own[-1], other[0] = down(own[0]), up(own[0]), across(own[0])
    ring = masked_ring(here, pattern, coupling)
    own[1], ring = tie((own[1], ring))
    own[2], other[1] = down(own[1]), across(own[1])
    own[-1], other[0] = tie((own[-1], other[0]))
    own[-2] = up(own[-1])
    own[3] = down(own[2])
    other[-2] = across(own[-2])
    own[-2], other[1] = tie((own[-2], other[1]))
    own[-3] = up(own[-2])
    other[-1] = up(other[0])
    other[2] = down(other[1])
    acc = add(0, -2, None)
    own[3], acc = tie((own[3], acc))
    own[4], other[3], other[4] = down(own[3]), across(own[3]), across_down(own[3])
    other[-3] = up(other[-2])
    acc = add(1, -2, acc)
    acc = add(0, 2, acc)
    result = add(1, 2, acc, last=True)

    back = lax.all_to_all(result, "mode", 0, 0, axis_index_groups=GROUPS, tiled=True)
    return small_call(unpack_kernel, flip, back, vectors.shape, (vmem, hbm), vectors.shape, (2,))


def solution(mesh):
    placed = (P(None, "wall", "mode"), P(None, None, "wall", None), P())
    return jax.shard_map(
        per_device, mesh=mesh, in_specs=placed, out_specs=P(None, "wall", "mode"), check_vma=False
    )
```
